256 devices in a mesh: blk: 16 (over z_hi, y, core), rep: 16 (over z_lo, x).
Axes of the slice: x: 4, y: 4, z: 8 (z_hi: 2, z_lo: 4; z = z_hi * 4 + z_lo), core: 2. Of those that a mesh axis runs over, the one named last changes fastest.
Arguments:
- query_rows: bfloat16 [114688, 2560], P(('blk', 'rep')), may hold values from -6 to 6
- key_rows: bfloat16 [114688, 2560], P(('blk', 'rep')), may hold values from -6 to 6
- value_rows: bfloat16 [114688, 2560], P(('blk', 'rep')), may hold values from -24 to 24
- cotangent: bfloat16 [114688, 2560], P(('blk', 'rep')), may hold values from -0.0625 to 0.0625
- out_weight: bfloat16 [2560, 2560], P('blk'), may hold values from -0.125 to 0.125
- first_moment: float32 [2560, 2560], P(('blk', 'rep')), may hold values from -6 to 6
- second_moment: float32 [2560, 2560], P(('blk', 'rep')), may hold values from 0.5 to 4
Outputs:
- projected: bfloat16 [114688, 2560], P(('blk', 'rep'))
- first_next: float32 [2560, 2560], P(('blk', 'rep'))
- second_next: float32 [2560, 2560], P(('blk', 'rep'))
The draws below stay inside these ranges and needn't reach their ends.
All inputs are finite; a program needn't handle non-finite values.
Results may differ from the reference program's by a relative error of at most 0.015.
Values may be sent and summed in bfloat16 or wider, within the bound.
A program may use at most 192 MiB of HBM per device.

```python
import math
import jax
import jax.numpy as jnp
from jax import lax

D = 2560
HEADS = 20
HD = 128
SEQ = 448
H = 2560
TOKENS = 114688


def drawn_pair(key):
    base = jax.random.fold_in(key, 4242)
    key_q, key_k = jax.random.split(base, 2)
    query_vals = jax.random.truncated_normal(key_q, -6.0, 6.0, (TOKENS, H), jnp.float32)
    key_vals = jax.random.truncated_normal(key_k, -6.0, 6.0, (TOKENS, H), jnp.float32)
    return (query_vals, key_vals)


def draw_query_rows(key, part):
    return drawn_pair(key)[0].astype(jnp.bfloat16)


def draw_key_rows(key, part):
    return drawn_pair(key)[1].astype(jnp.bfloat16)


def strengthened(entries, stream_key, source, target, blocks, factor):
    owner, partner = [(jnp.arange(entries.shape[position]) // (entries.shape[position] // blocks)).reshape([-1 if axis == position else 1 for axis in range(entries.ndim)]) for position in (source, target)]
    chosen = jax.random.permutation(stream_key, blocks)[partner]
    strong = (owner == chosen) | (owner == (partner + blocks // 2) % blocks)
    return jnp.where(strong, factor * entries, entries)


def shard_levels(own_key, shape, cuts, low, high):
    def one(dim, blocks):
        heights = jax.random.uniform(jax.random.fold_in(jax.random.fold_in(own_key, 6), dim), (blocks,), jnp.float32, low / len(cuts), high / len(cuts))
        return jnp.repeat(jnp.exp(heights), shape[dim] // blocks).reshape((-1,) + (1,) * (len(shape) - dim - 1))

    factor_of = one(*cuts[0])
    for cut in cuts[1:]:
        factor_of = factor_of * one(*cut)
    return factor_of


def scatter_about(key, shape, spread, reach, cuts=(), dtype=jnp.bfloat16):
    level = shard_levels(key, shape, cuts, -0.22, 0.18) if cuts else 1.0
    values = jax.random.normal(key, shape, jnp.float32) * spread * level
    return jnp.minimum(jnp.maximum(values, -reach), reach).astype(dtype)


def bell_draw_with(rng, shape, width, limit, shards, heavy, kind=jnp.bfloat16):
    drawn = width * jax.random.normal(rng, shape, jnp.float32)
    if shards:
        drawn = drawn * shard_levels(rng, shape, shards, -0.22, 0.18)
    return jnp.clip(strengthened(drawn, jax.random.fold_in(rng, 3), *heavy), -limit, limit).astype(kind)


def setup_inputs(seed: int = 0) -> dict:
    seeds = jax.random.split(jax.random.key(seed), 8)
    return {
        "query_rows": draw_query_rows(jax.random.fold_in(seeds[7], 71), 0),
        "key_rows": draw_key_rows(jax.random.fold_in(seeds[7], 71), 0),
        "value_rows": bell_draw_with(seeds[2], (TOKENS, H), 1.0, 24.0, ((0, 256),), (0, 1, 256, 6.0)),
        "cotangent": scatter_about(seeds[3], (TOKENS, D), (TOKENS // 16) ** -0.5, 0.0625, ((0, 256),)),
        "out_weight": scatter_about(seeds[4], (H, D), H ** -0.5, 0.125, ((0, 16),)),
        "first_moment": scatter_about(seeds[5], (H, D), 1.0, 6.0, ((0, 256),), jnp.float32),
        "second_moment": jnp.clip(jnp.exp(math.log(4.0) - 2.0794415 * jax.random.uniform(seeds[6], (H, D), jnp.float32) ** shard_levels(seeds[6], (H, D), ((0, 256),), -0.2, 0.2)), 0.5, 4.0),
    }


NEG = -1e+30

def attend(query_part, key_part, value_part):
    length = query_part.shape[0]
    q = query_part.reshape(length, HEADS, HD).astype(jnp.float32)
    k = key_part.reshape(length, HEADS, HD).astype(jnp.float32)
    v = value_part.reshape(length, HEADS, HD).astype(jnp.float32)
    scores = jnp.einsum('qhd,khd->hqk', q, k) * (1.0 / math.sqrt(HD))
    later = lax.broadcasted_iota(jnp.int32, (length, length), 1) > lax.broadcasted_iota(jnp.int32, (length, length), 0)
    scores = jnp.where(later[None, :, :], NEG, scores)
    top = lax.optimization_barrier(jnp.max(scores, axis=-1, keepdims=True))
    expo = jnp.exp(scores - top)
    probs = (expo / lax.optimization_barrier(jnp.sum(expo, axis=-1, keepdims=True))).astype(jnp.bfloat16)
    context = jnp.einsum('hqk,khd->qhd', probs.astype(jnp.float32), v)
    return context.reshape(length, HEADS * HD).astype(jnp.bfloat16)

def reference(query_rows, key_rows, value_rows, cotangent, out_weight, first_moment, second_moment):
    count = TOKENS // SEQ
    stacked = (query_rows.reshape(count, SEQ, H), key_rows.reshape(count, SEQ, H), value_rows.reshape(count, SEQ, H), cotangent.reshape(count, SEQ, D))

    def one_sequence(total, pieces):
        query_part, key_part, value_part, grad_part = pieces
        context = attend(query_part, key_part, value_part)
        proj = jnp.dot(context, out_weight, preferred_element_type=jnp.float32).astype(jnp.bfloat16)
        term = lax.dot_general(context, grad_part, (((0,), (0,)), ((), ())), preferred_element_type=jnp.float32)
        term = lax.optimization_barrier(term.astype(jnp.bfloat16)).astype(jnp.float32)
        return (total + term, proj)
    gradient, projs = lax.scan(one_sequence, jnp.zeros((H, D), jnp.float32), stacked)
    first_next = 0.9 * first_moment + 0.1 * gradient
    second_next = 0.95 * second_moment + 0.05 * gradient * gradient
    return (projs.reshape(TOKENS, D), first_next, second_next)
```

```python
import functools
import math

import jax
import jax.numpy as jnp
from jax import lax
from jax.experimental import pallas as pl
from jax.experimental.pallas import tpu as pltpu
from jax.sharding import PartitionSpec as P

HEADS = 20
HD = 128
SEQ = 448
D = 2560
NEG = -1e30
BF = jnp.bfloat16
F32 = jnp.float32
MESH = pl.DeviceIdType.MESH
WA, WB, WC = 48, 32, 80
Q4 = D // 4
NSEM = 110
SCALE = math.log2(math.e) / math.sqrt(HD)
QBLOCKS = ((0, 128), (128, 128), (256, 128), (384, 64))


def ring(value, shift, size):
    return lax.rem(value + shift + size, size)


def kernel(q_hbm, k_hbm, v_hbm, t_hbm, w_hbm, m1_hbm, m2_hbm,
           out_hbm, first_hbm, second_hbm,
           qs, ks, vs, ct, cto, ctx, ctt, cxo, wf, go, r1x, r2x, r1y, r2y, r3a, r3b, pc, rz, s3, snd, r4,
           m1, m2, ss, rs, ls):
    blk = lax.axis_index("blk")
    rep = lax.axis_index("rep")
    zh, y, c = blk // 8, lax.rem(blk // 2, 4), lax.rem(blk, 2)
    zl, x = rep // 4, lax.rem(rep, 4)
    z = zh * 4 + zl
    oz, oc = 1 - zh, 1 - c

    def at(xx, yy, zz, cc):
        return (zz // 4) * 8 + yy * 2 + cc, lax.rem(zz, 4) * 4 + xx

    def dx(s):
        return at(ring(x, s, 4), y, z, c)

    def dy(s):
        return at(x, ring(y, s, 4), z, c)

    def dz(s):
        return at(x, y, ring(z, s, 8), c)

    sib = at(x, y, z, oc)

    count = [0]
    sent = []

    def send(src, dst, dev):
        i = count[0]
        count[0] += 1
        cp = pltpu.make_async_remote_copy(
            src_ref=src, dst_ref=dst, send_sem=ss.at[i], recv_sem=rs.at[i],
            device_id=dev, device_id_type=MESH)
        cp.start()
        sent.append(cp)
        return cp

    def local(i, src, dst):
        cp = pltpu.make_async_copy(src, dst, ls.at[i])
        cp.start()
        return cp

    lw = local(0, w_hbm, wf.at[zh, y, c])
    lt = local(1, t_hbm, ct)
    lq = local(2, q_hbm, qs)
    lk = local(3, k_hbm, ks)
    lv = local(4, v_hbm, vs)
    lm1 = local(5, m1_hbm, m1)
    lm2 = local(6, m2_hbm, m2)

    lw.wait()
    barrier = pltpu.get_barrier_semaphore()
    partners = [dx(1), dx(2), dx(3), dy(1), dy(2), dy(3)] + [dz(s) for s in range(1, 8)] + [sib]
    for dev in partners:
        pl.semaphore_signal(barrier, inc=1, device_id=dev, device_id_type=MESH)
    pl.semaphore_wait(barrier, len(partners))

    def cols(quarter):
        return pl.ds(pl.multiple_of(quarter * Q4, 128), Q4)

    ra, rb, rc = pl.ds(0, WA), pl.ds(WA, WB), pl.ds(WA + WB, WC)

    def give(dev, *region):
        ref = wf.at[region]
        return send(ref, ref, dev)

    c1 = [give(dy(s), zh, y, c, rc, cols(zl)) for s in (1, 3, 2)]
    a1 = give(dz(4), zh, y, c, pl.ds(0, WA + WB), cols(x))
    a2o = [give(dy(s), zh, y, c, ra, cols(x)) for s in (1, 3, 2)]
    b3o = [give(dy(1), zh, y, c, rb, pl.ds(0, D)), give(dy(3), zh, y, c, rb, pl.ds(0, D))]
    lt.wait()
    tsend = send(ct, cto, sib)
    lq.wait()
    lk.wait()
    lv.wait()

    def attend(h, carry):
        off = pl.multiple_of(h * HD, HD)
        lane = pl.ds(off, HD)
        for q0, qn in QBLOCKS:
            kn = q0 + qn
            s = lax.dot_general(qs[pl.ds(q0, qn), lane], ks[pl.ds(0, kn), lane],
                                (((1,), (1,)), ((), ())), preferred_element_type=F32)
            later = lax.broadcasted_iota(jnp.int32, (qn, kn), 1) > lax.broadcasted_iota(
                jnp.int32, (qn, kn), 0) + q0
            s = jnp.where(later, NEG, s)
            top = jnp.max(s, axis=-1, keepdims=True)
            p = jnp.exp2((s - top) * SCALE)
            total = jnp.sum(p, axis=-1, keepdims=True)
            o = lax.dot_general(p.astype(BF), vs[pl.ds(0, kn), lane],
                                (((1,), (0,)), ((), ())), preferred_element_type=F32)
            o = o * (1.0 / total)
            ctx[pl.ds(q0, qn), lane] = o.astype(BF)
            ctt[pl.ds(off, HD), pl.ds(q0, qn)] = o.T.astype(BF)
        return carry

    def heads(lo, hi):
        lax.fori_loop(lo, hi, attend, 0)

    def rows_of(zz, yy, cc):
        return pl.ds(pl.multiple_of((zz * 8 + yy * 2 + cc) * 160, 32), 160)

    heads(0, 5)
    for cp in c1:
        cp.wait_recv()
    every = pl.ds(0, 4)
    c2 = [[give(dz(1), zh, every, c, rc, cols(zl)), give(dz(7), zh, every, c, rc, cols(zl))]]
    sibs = [give(sib, zh, every, c, rc, cols(zl))]
    a1.wait_recv()
    b2 = [give(dx(s), oz, y, c, rb, cols(x)) for s in (1, 3, 2)]
    a2t = [give(dy(s), oz, y, c, ra, cols(x)) for s in (1, 3, 2)]
    heads(5, 10)
    for cp in a2o:
        cp.wait_recv()
    a3o = [give(dx(1), zh, every, c, ra, cols(x)), give(dx(3), zh, every, c, ra, cols(x))]
    for cp in b2:
        cp.wait_recv()
    b3t = [give(dy(1), oz, y, c, rb, pl.ds(0, D)), give(dy(3), oz, y, c, rb, pl.ds(0, D))]
    heads(10, 15)
    half = (pl.ds(0, D // 2), pl.ds(D // 2, D // 2))
    b3o[0].wait_recv()
    fo = [give(dy(1), zh, ring(y, -1, 4), c, rb, half[0])]
    b3o[1].wait_recv()
    fo.append(give(dy(3), zh, ring(y, 1, 4), c, rb, half[1]))

    def zpos(s):
        zz = ring(z, s, 8)
        return zz // 4, lax.rem(zz, 4)

    def zstep(step):
        prev = c2[step - 1]
        nxt = []
        for side, cp in enumerate(prev):
            cp.wait_recv()
            hh, ll = zpos(-step if side == 0 else step)
            if step < 3:
                part = every
            else:
                part = pl.ds(0, 2) if side == 0 else pl.ds(2, 2)
            nxt.append(give(dz(1 if side == 0 else 7), hh, part, c, rc, cols(ll)))
            sibs.append(give(sib, hh, every, c, rc, cols(ll)))
        c2.append(nxt)

    zstep(1)
    heads(15, 20)
    xs = [send(ctt.at[rows_of(zz, yy, oc)], cxo.at[zz, yy], sib) for zz in range(2) for yy in range(4)]
    for cp in a2t:
        cp.wait_recv()
    a3t = [give(dx(1), oz, every, c, ra, cols(x)), give(dx(3), oz, every, c, ra, cols(x))]
    for cp in b3t:
        cp.wait_recv()
    ft = [give(dy(1), oz, ring(y, -1, 4), c, rb, half[0]), give(dy(3), oz, ring(y, 1, 4), c, rb, half[1])]

    tsend.wait_recv()

    xp, xo, xm = ring(x, 1, 4), ring(x, 2, 4), ring(x, 3, 4)
    yp, yo, ym = ring(y, 1, 4), ring(y, 2, 4), ring(y, 3, 4)
    ga, gb = pl.ds(0, 80), pl.ds(80, 80)
    alld = pl.ds(0, D)

    def grads(zz):
        for cp in xs[zz * 4:zz * 4 + 4]:
            cp.wait_recv()

        def tile(n, carry):
            lane = pl.ds(pl.multiple_of(n * 512, 128), 512)
            mine = jnp.concatenate([ctt[rows_of(zz, yy, c), :] for yy in range(4)], axis=0)
            acc = jnp.dot(mine, ct[:, lane], preferred_element_type=F32)
            acc += jnp.dot(cxo[zz].reshape(640, SEQ), cto[:, lane], preferred_element_type=F32)
            go[zz, :, :, lane] = acc.astype(BF).reshape(4, 160, 512)
            return carry

        lax.fori_loop(0, 5, tile, 0)

    grads(0)
    s1xp = send(go.at[0, every, ga, cols(xo)], r1x.at[0], dx(1))
    s1yp = send(go.at[0, yo, gb, alld], r1y.at[0], dy(1))
    oxm = send(go.at[0, every, ga, cols(xm)], r2x.at[1, 0], dx(3))
    oym = send(go.at[0, ym, gb, alld], r2y.at[1, 0], dy(3))
    a3o[0].wait_recv()
    fa = []
    ah = (pl.ds(0, 2), pl.ds(2, 2))
    fa.append(give(dx(1), zh, ah[0], c, ra, cols(xm)))
    a3o[1].wait_recv()
    fa.append(give(dx(3), zh, ah[1], c, ra, cols(xp)))
    grads(1)
    s1xm = send(go.at[1, every, ga, cols(xo)], r1x.at[1], dx(3))
    s1ym = send(go.at[1, yo, gb, alld], r1y.at[1], dy(3))
    oxp = send(go.at[1, every, ga, cols(xp)], r2x.at[0, 1], dx(1))
    oyp = send(go.at[1, yp, gb, alld], r2y.at[0, 1], dy(1))

    zstep(2)
    for cp in fo:
        cp.wait_recv()
    sibs.append(give(sib, zh, every, c, rb, alld))
    for cp in ft:
        cp.wait_recv()
    sibs.append(give(sib, oz, every, c, rb, alld))
    a3t[0].wait_recv()
    fa.append(give(dx(1), oz, ah[0], c, ra, cols(xm)))
    a3t[1].wait_recv()
    fa.append(give(dx(3), oz, ah[1], c, ra, cols(xp)))

    def addf(*parts):
        total = parts[0].astype(F32)
        for part in parts[1:]:
            total = total + part.astype(F32)
        return total.astype(BF)

    s1xp.wait_recv()
    for yy in range(4):
        go[0, yy, ga, cols(xp)] = addf(go[0, yy, ga, cols(xp)], r1x[0, yy])
    s2xp = send(go.at[0, every, ga, cols(xp)], r2x.at[0, 0], dx(1))
    s1yp.wait_recv()
    go[0, yp, gb, :] = addf(go[0, yp, gb, :], r1y[0])
    s2yp = send(go.at[0, yp, gb, alld], r2y.at[0, 0], dy(1))
    s1xm.wait_recv()
    for yy in range(4):
        go[1, yy, ga, cols(xm)] = addf(go[1, yy, ga, cols(xm)], r1x[1, yy])
    s2xm = send(go.at[1, every, ga, cols(xm)], r2x.at[1, 1], dx(3))
    s1ym.wait_recv()
    go[1, ym, gb, :] = addf(go[1, ym, gb, :], r1y[1])
    s2ym = send(go.at[1, ym, gb, alld], r2y.at[1, 1], dy(3))

    for cp in fa:
        cp.wait_recv()
    sibs.append(give(sib, zh, every, c, ra, alld))
    sibs.append(give(sib, oz, every, c, ra, alld))
    zstep(3)
    for cp in c2[3]:
        cp.wait_recv()
    hh, ll = zpos(4)
    sibs.append(give(sib, hh, every, c, rc, cols(ll)))
    for cp in sibs:
        cp.wait_recv()

    outs = []
    for n in range(10):
        lane = pl.ds(n * 256, 256)
        w = wf[:, :, :, :, lane].reshape(D, 256)
        qs[:, lane] = jnp.dot(ctx[...], w, preferred_element_type=F32).astype(BF)
    outs.append(local(7, qs, out_hbm))

    for cp in (oxm, oxp, s2xp, s2xm):
        cp.wait_recv()
    for zz in range(2):
        for yy in range(4):
            go[zz, yy, ga, cols(x)] = addf(go[zz, yy, ga, cols(x)], r2x[0, zz, yy], r2x[1, zz, yy])
    both = pl.ds(0, 2)
    p2a = [send(go.at[both, ring(y, s, 4), ga, cols(x)], r3a.at[s - 1], dy(s)) for s in (1, 3, 2)]
    for cp in (oym, oyp, s2yp, s2ym):
        cp.wait_recv()
    for zz in range(2):
        go[zz, y, gb, :] = addf(go[zz, y, gb, :], r2y[0, zz], r2y[1, zz])
    p2b = [send(go.at[both, y, gb, cols(ring(x, s, 4))], r3b.at[s - 1], dx(s)) for s in (1, 3, 2)]
    for cp in p2a:
        cp.wait_recv()
    for zz in range(2):
        pc[zz, ga, :] = addf(go[zz, y, ga, cols(x)], r3a[0, zz], r3a[1, zz], r3a[2, zz])
    for cp in p2b:
        cp.wait_recv()
    for zz in range(2):
        pc[zz, gb, :] = addf(go[zz, y, gb, cols(x)], r3b[0, zz], r3b[1, zz], r3b[2, zz])

    def window(ll):
        return pl.ds(pl.multiple_of(ll * 40 - 8 * lax.rem(ll, 2), 16), 48)

    p3 = []
    for s in (4, 3, 5, 2, 6, 1, 7):
        hh, ll = zpos(s)
        p3.append(send(pc.at[hh, window(ll), :], rz.at[s - 1], dz(s)))
    for cp in p3:
        cp.wait_recv()
    total = pc[zh, window(zl), :].astype(F32)
    for s in range(7):
        total = total + rz[s].astype(F32)
    s3[...] = total

    mine = s3[pl.ds(pl.multiple_of(8 * lax.rem(zl, 2), 8), 40), :]
    snd[...] = jnp.zeros(snd.shape, F32)
    for t in range(4):
        snd[t, pl.ds(0, 10), :] = mine[10 * t:10 * t + 10, :]
    p4 = [send(snd.at[ring(x, s, 4)], r4.at[s - 1], dx(s)) for s in (1, 3, 2)]
    lm1.wait()
    lm2.wait()

    def adam(quarter, g):
        lane = cols(quarter)
        m1[:, lane] = 0.9 * m1[:, lane] + 0.1 * g
        m2[:, lane] = 0.95 * m2[:, lane] + 0.05 * g * g

    adam(x, snd[x, pl.ds(0, 10), :])
    for s, cp in zip((1, 3, 2), p4):
        cp.wait_recv()
        adam(ring(x, -s, 4), r4[s - 1, pl.ds(0, 10), :])
    outs.append(local(8, m1, first_hbm))
    outs.append(local(9, m2, second_hbm))
    for cp in sent:
        cp.wait_send()
    for cp in outs:
        cp.wait()
    assert count[0] <= NSEM, count[0]


def on_device(*args):
    any_spec = pl.BlockSpec(memory_space=pl.ANY)
    V = pltpu.VMEM
    return pl.pallas_call(
        kernel,
        name="fused_layer",
        out_shape=(
            jax.ShapeDtypeStruct((SEQ, D), BF),
            jax.ShapeDtypeStruct((10, D), F32),
            jax.ShapeDtypeStruct((10, D), F32),
        ),
        in_specs=[any_spec] * 7,
        out_specs=(any_spec,) * 3,
        scratch_shapes=[
            V((SEQ, D), BF), V((SEQ, D), BF), V((SEQ, D), BF), V((SEQ, D), BF), V((SEQ, D), BF),
            V((SEQ, D), BF),
            V((D, SEQ), BF),
            V((2, 4, 160, SEQ), BF),
            V((2, 4, 2, 160, D), BF),
            V((2, 4, 160, D), BF),
            V((2, 4, 80, Q4), BF),
            V((2, 2, 4, 80, Q4), BF),
            V((2, 80, D), BF),
            V((2, 2, 80, D), BF),
            V((3, 2, 80, Q4), BF),
            V((3, 2, 80, Q4), BF),
            V((2, 160, Q4), BF),
            V((7, 48, Q4), BF),
            V((48, Q4), F32),
            V((4, 16, Q4), F32),
            V((3, 16, Q4), F32),
            V((10, D), F32), V((10, D), F32),
            pltpu.SemaphoreType.DMA((NSEM,)),
            pltpu.SemaphoreType.DMA((NSEM,)),
            pltpu.SemaphoreType.DMA((10,)),
        ],
        compiler_params=pltpu.CompilerParams(
            collective_id=0, has_side_effects=True, vmem_limit_bytes=60 * 2**20),
        cost_estimate=pl.CostEstimate(flops=15_000_000_000, bytes_accessed=14_000_000, transcendentals=2_600_000),
    )(*args)


def solution(mesh):
    rows = P(("blk", "rep"), None)
    return jax.shard_map(
        on_device, mesh=mesh, in_specs=(rows, rows, rows, rows, P("blk", None), rows, rows),
        out_specs=(rows, rows, rows), check_vma=False)
```

```python
import functools
import math

import jax
import jax.numpy as jnp
from jax import lax
from jax.experimental import pallas as pl
from jax.experimental.pallas import tpu as pltpu
from jax.sharding import PartitionSpec as P

HEADS = 20
HD = 128
SEQ = 448
D = 2560
NEG = -1e30
BF = jnp.bfloat16
F32 = jnp.float32
MESH = pl.DeviceIdType.MESH
WA, WB, WC = 32, 16, (64, 48)
Q4 = D // 4
NSEM = 160
CHUNKS = ((0, 48), (48, 32))
SCALE = math.log2(math.e) / math.sqrt(HD)
QBLOCKS = ((0, 256), (256, 192))


def ring(value, shift, size):
    return lax.rem(value + shift + size, size)


def kernel(q_hbm, k_hbm, v_hbm, t_hbm, w_hbm, m1_hbm, m2_hbm,
           out_ref, first_ref, second_ref,
           qs, ks, vs, ct, cto, ctx, ctt, cxo, wf, go, r1x, r2x, r1y, r2y, r3a, r3b, pc, rz, s3, snd, r4,
           m1, m2, ss, rs, ls):
    blk = lax.axis_index("blk")
    rep = lax.axis_index("rep")
    zh, y, c = blk // 8, lax.rem(blk // 2, 4), lax.rem(blk, 2)
    zl, x = rep // 4, lax.rem(rep, 4)
    z = zh * 4 + zl
    oz, oc = 1 - zh, 1 - c

    def at(xx, yy, zz, cc):
        return (zz // 4) * 8 + yy * 2 + cc, lax.rem(zz, 4) * 4 + xx

    def dx(s):
        return at(ring(x, s, 4), y, z, c)

    def dy(s):
        return at(x, ring(y, s, 4), z, c)

    def dz(s):
        return at(x, y, ring(z, s, 8), c)

    sib = at(x, y, z, oc)

    count = [0]
    sent = []

    def send(src, dst, dev):
        i = count[0]
        count[0] += 1
        cp = pltpu.make_async_remote_copy(
            src_ref=src, dst_ref=dst, send_sem=ss.at[i], recv_sem=rs.at[i],
            device_id=dev, device_id_type=MESH)
        cp.start()
        sent.append(cp)
        return cp

    def local(i, src, dst):
        cp = pltpu.make_async_copy(src, dst, ls.at[i])
        cp.start()
        return cp

    lw = local(0, w_hbm, wf.at[zh, y, c])
    lt = local(1, t_hbm, ct)
    lq = local(2, q_hbm, qs)
    lk = local(3, k_hbm, ks)
    lv = local(4, v_hbm, vs)
    lm1 = local(5, m1_hbm, m1)
    lm2 = local(6, m2_hbm, m2)

    lw.wait()
    barrier = pltpu.get_barrier_semaphore()
    partners = [dx(1), dx(2), dx(3), dy(1), dy(2), dy(3)] + [dz(s) for s in range(1, 8)] + [sib]
    for dev in partners:
        pl.semaphore_signal(barrier, inc=1, device_id=dev, device_id_type=MESH)
    pl.semaphore_wait(barrier, len(partners))

    def cols(quarter):
        return pl.ds(pl.multiple_of(quarter * Q4, 128), Q4)

    ra, rb = pl.ds(0, WA), pl.ds(WA, WB)
    rc = (pl.ds(WA + WB, WC[0]), pl.ds(WA + WB + WC[0], WC[1]))

    def give(dev, *region):
        ref = wf.at[region]
        return send(ref, ref, dev)

    a2o = [give(dy(s), zh, y, c, ra, cols(x)) for s in (1, 3, 2)]
    a1 = give(dz(4), zh, y, c, pl.ds(0, WA + WB), cols(x))
    c1 = [[give(dy(s), zh, y, c, rc[0], cols(zl)) for s in (1, 3, 2)]]
    b3o = [give(dy(1), zh, y, c, rb, pl.ds(0, D)), give(dy(3), zh, y, c, rb, pl.ds(0, D))]
    c1.append([give(dy(s), zh, y, c, rc[1], cols(zl)) for s in (1, 3, 2)])
    lt.wait()
    tsend = send(ct, cto, sib)
    lq.wait()
    lk.wait()
    lv.wait()

    def attend(i, carry):
        work = []
        for j in range(4):
            off = pl.multiple_of((i * 4 + j) * HD, HD)
            for q0, qn in QBLOCKS:
                work.append((off, pl.ds(off, HD), q0, qn, q0 + qn))
        scores = []
        for off, lane, q0, qn, kn in work:
            s = lax.dot_general(ks[pl.ds(0, kn), lane], qs[pl.ds(q0, qn), lane],
                                (((1,), (1,)), ((), ())), preferred_element_type=F32)
            later = lax.broadcasted_iota(jnp.int32, (qn, qn), 0) > lax.broadcasted_iota(
                jnp.int32, (qn, qn), 1)
            last = jnp.where(later, NEG, s[q0:])
            scores.append(jnp.concatenate([s[:q0], last], axis=0) if q0 else last)
        probs = []
        for s in scores:
            p = jnp.exp2((s - jnp.max(s, axis=0, keepdims=True)) * SCALE)
            probs.append((p.astype(BF), 1.0 / jnp.sum(p, axis=0, keepdims=True)))
        for (off, lane, q0, qn, kn), (p, inv) in zip(work, probs):
            o = inv * lax.dot_general(vs[pl.ds(0, kn), lane], p,
                                      (((0,), (0,)), ((), ())), preferred_element_type=F32)
            ctt[pl.ds(off, HD), pl.ds(q0, qn)] = o.astype(BF)
            ctx[pl.ds(q0, qn), lane] = o.T.astype(BF)
        return carry

    def heads(lo, hi):
        lax.fori_loop(lo // 4, hi // 4, attend, 0)

    def rows_of(zz, yy, cc):
        return pl.ds(pl.multiple_of((zz * 8 + yy * 2 + cc) * 160, 32), 160)

    every, both = pl.ds(0, 4), pl.ds(0, 2)
    halves = (pl.ds(0, D // 2), pl.ds(D // 2, D // 2))
    ah = (pl.ds(0, 2), pl.ds(2, 2))
    xp, xo, xm = ring(x, 1, 4), ring(x, 2, 4), ring(x, 3, 4)
    yp, yo, ym = ring(y, 1, 4), ring(y, 2, 4), ring(y, 3, 4)
    alld = pl.ds(0, D)
    sibs = []

    def zpos(s):
        zz = ring(z, s, 8)
        return zz // 4, lax.rem(zz, 4)

    c2 = [[], []]

    def zstep(step, strand):
        nxt = []
        for side in range(2):
            hh, ll = zpos(-step if side == 0 else step)
            if step:
                c2[strand][step - 1][side].wait_recv()
            if step < 4:
                part = ah[side] if step == 3 else every
                nxt.append(give(dz(1 if side == 0 else 7), hh, part, c, rc[strand], cols(ll)))
            if side == 0 or 0 < step < 4:
                if step < 4:
                    sibs.append(give(sib, hh, every, c, rc[strand], cols(ll)))
        if step == 4:
            hh, ll = zpos(4)
            sibs.append(give(sib, hh, every, c, rc[strand], cols(ll)))
        c2[strand].append(nxt)

    xs = []

    def context_across(blocks):
        for b in blocks:
            zz, yy = b // 4, b % 4
            xs.append(send(ctt.at[rows_of(zz, yy, oc)], cxo.at[zz, yy], sib))

    def grads(zz):
        for cp in xs[zz * 4:zz * 4 + 4]:
            cp.wait_recv()

        def tile(n, carry):
            lane = pl.ds(pl.multiple_of(n * 512, 128), 512)
            mine = jnp.concatenate([ctt[rows_of(zz, yy, c), :] for yy in range(4)], axis=0)
            acc = jnp.dot(mine, ct[:, lane], preferred_element_type=F32)
            acc += jnp.dot(cxo[zz].reshape(640, SEQ), cto[:, lane], preferred_element_type=F32)
            go[zz, :, :, lane] = acc.astype(BF).reshape(4, 160, 512)
            return carry

        lax.fori_loop(0, 5, tile, 0)

    def addf(*parts):
        total = parts[0].astype(F32)
        for part in parts[1:]:
            total = total + part.astype(F32)
        return total.astype(BF)

    s1, own, s2 = {}, {}, {}
    spans = [(pl.ds(lo, n), pl.ds(80 + lo, n)) for lo, n in CHUNKS]

    def first(k, zz):
        ga, gb = spans[k]
        fwd, back = (1, 3) if zz == 0 else (3, 1)
        bx, by = ring(x, back, 4), ring(y, back, 4)
        s1[k, zz] = (
            send(go.at[zz, every, ga, cols(xo)], r1x.at[zz, every, ga], dx(fwd)),
            send(go.at[zz, yo, gb, alld], r1y.at[zz, ga], dy(fwd)))
        own[k, zz] = (
            send(go.at[zz, every, ga, cols(bx)], r2x.at[1 - zz, zz, every, ga], dx(back)),
            send(go.at[zz, by, gb, alld], r2y.at[1 - zz, zz, ga], dy(back)))

    def second(k, zz):
        ga, gb = spans[k]
        fwd = 1 if zz == 0 else 3
        fx, fy = ring(x, fwd, 4), ring(y, fwd, 4)
        s1[k, zz][0].wait_recv()
        for yy in range(4):
            go[zz, yy, ga, cols(fx)] = addf(go[zz, yy, ga, cols(fx)], r1x[zz, yy, ga])
        a = send(go.at[zz, every, ga, cols(fx)], r2x.at[zz, zz, every, ga], dx(fwd))
        s1[k, zz][1].wait_recv()
        go[zz, fy, gb, :] = addf(go[zz, fy, gb, :], r1y[zz, ga])
        b = send(go.at[zz, fy, gb, alld], r2y.at[zz, zz, ga], dy(fwd))
        s2[k, zz] = (a, b)

    p2 = {}

    def third(k):
        ga, gb = spans[k]
        for zz in range(2):
            own[k, zz][0].wait_recv()
            s2[k, zz][0].wait_recv()
            for yy in range(4):
                go[zz, yy, ga, cols(x)] = addf(go[zz, yy, ga, cols(x)], r2x[0, zz, yy, ga], r2x[1, zz, yy, ga])
        pa = [send(go.at[both, ring(y, s, 4), ga, cols(x)], r3a.at[s - 1, both, ga], dy(s)) for s in (1, 3, 2)]
        for zz in range(2):
            own[k, zz][1].wait_recv()
            s2[k, zz][1].wait_recv()
            go[zz, y, gb, :] = addf(go[zz, y, gb, :], r2y[0, zz, ga], r2y[1, zz, ga])
        pb = [send(go.at[both, y, gb, cols(ring(x, s, 4))], r3b.at[s - 1, both, ga], dx(s)) for s in (1, 3, 2)]
        p2[k] = (pa, pb)

    def fourth(k):
        ga, gb = spans[k]
        for cp in p2[k][0]:
            cp.wait_recv()
        for zz in range(2):
            pc[zz, ga, :] = addf(go[zz, y, ga, cols(x)], *[r3a[s, zz, ga] for s in range(3)])
        for cp in p2[k][1]:
            cp.wait_recv()
        for zz in range(2):
            pc[zz, gb, :] = addf(go[zz, y, gb, cols(x)], *[r3b[s, zz, ga] for s in range(3)])

    par = lax.rem(z, 2)
    zbase = NSEM - 8

    def window(ll):
        return pl.ds(pl.multiple_of(ll * 40 - 8 * lax.rem(ll, 2), 16), 48)

    def along_z(i, odd):
        zz = lax.rem(z // 2 + i, 4) * 2 + odd
        hh, ll = zz // 4, lax.rem(zz, 4)
        slot = 2 * i + par
        return pltpu.make_async_remote_copy(
            src_ref=pc.at[hh, window(ll), :], dst_ref=rz.at[slot],
            send_sem=ss.at[zbase + 2 * i + odd], recv_sem=rs.at[zbase + slot],
            device_id=at(x, y, zz, c), device_id_type=MESH)

    def wave(odd):
        for i in (2, 1, 3):
            along_z(i, odd).start()

        @pl.when(par != odd)
        def _():
            along_z(0, odd).start()

    heads(0, 8)
    context_across([0, 1, 2])
    heads(8, 12)
    context_across([3])
    for cp in a2o:
        cp.wait_recv()
    a3o = [give(dx(1), zh, every, c, ra, cols(x)), give(dx(3), zh, every, c, ra, cols(x))]
    a1.wait_recv()
    a2t = [give(dy(s), oz, y, c, ra, cols(x)) for s in (1, 3, 2)]
    b2 = [give(dx(s), oz, y, c, rb, cols(x)) for s in (1, 3, 2)]
    tsend.wait_recv()
    grads(0)
    first(0, 0)
    for strand in range(2):
        for cp in c1[strand]:
            cp.wait_recv()
        zstep(0, strand)
    heads(12, 20)
    context_across([4, 5, 6, 7])
    for cp in b2:
        cp.wait_recv()
    b3t = [give(dy(1), oz, y, c, rb, alld), give(dy(3), oz, y, c, rb, alld)]
    b3o[0].wait_recv()
    fo = [give(dy(1), zh, ym, c, rb, halves[0])]
    b3o[1].wait_recv()
    fo.append(give(dy(3), zh, yp, c, rb, halves[1]))
    grads(1)
    first(0, 1)
    for cp in a2t:
        cp.wait_recv()
    a3t = [give(dx(1), oz, every, c, ra, cols(x)), give(dx(3), oz, every, c, ra, cols(x))]
    zstep(1, 0)
    a3o[0].wait_recv()
    fa = [give(dx(1), zh, ah[0], c, ra, cols(xm))]
    a3o[1].wait_recv()
    fa.append(give(dx(3), zh, ah[1], c, ra, cols(xp)))
    first(1, 0)
    second(0, 0)
    zstep(1, 1)
    second(0, 1)
    first(1, 1)
    for cp in b3t:
        cp.wait_recv()
    ft = [give(dy(1), oz, ym, c, rb, halves[0]), give(dy(3), oz, yp, c, rb, halves[1])]
    for cp in fo:
        cp.wait_recv()
    sibs.append(give(sib, zh, every, c, rb, alld))
    a3t[0].wait_recv()
    fa.append(give(dx(1), oz, ah[0], c, ra, cols(xm)))
    a3t[1].wait_recv()
    fa.append(give(dx(3), oz, ah[1], c, ra, cols(xp)))
    zstep(2, 0)
    second(1, 0)
    zstep(2, 1)
    second(1, 1)
    third(0)
    zstep(3, 0)
    for cp in ft:
        cp.wait_recv()
    sibs.append(give(sib, oz, every, c, rb, alld))
    for cp in fa:
        cp.wait_recv()
    sibs.append(give(sib, zh, every, c, ra, alld))
    sibs.append(give(sib, oz, every, c, ra, alld))
    zstep(3, 1)
    third(1)
    fourth(0)
    wave(0)
    zstep(4, 0)
    fourth(1)
    wave(1)
    zstep(4, 1)

    for cp in sibs:
        cp.wait_recv()
    for n in range(10):
        lane = pl.ds(n * 256, 256)
        w = wf[:, :, :, :, lane].reshape(D, 256)
        out_ref[:, lane] = jnp.dot(ctx[...], w, preferred_element_type=F32).astype(BF)

    for i in (1, 3, 2):
        for sender in range(2):
            pltpu.make_async_remote_copy(
                src_ref=rz.at[0], dst_ref=rz.at[2 * i + sender], send_sem=ss.at[zbase],
                recv_sem=rs.at[zbase + 2 * i + sender], device_id=dz(1), device_id_type=MESH).wait_recv()
    pltpu.make_async_remote_copy(
        src_ref=rz.at[0], dst_ref=rz.at[1 - par], send_sem=ss.at[zbase],
        recv_sem=rs.at[zbase + 1 - par], device_id=dz(1), device_id_type=MESH).wait_recv()
    total = pc[zh, window(zl), :].astype(F32) + rz[1 - par].astype(F32)
    for slot in range(2, 8):
        total = total + rz[slot].astype(F32)
    s3[...] = total

    mine = s3[pl.ds(pl.multiple_of(8 * lax.rem(zl, 2), 8), 40), :]
    snd[...] = jnp.zeros(snd.shape, F32)
    for t in range(4):
        snd[t, pl.ds(0, 10), :] = mine[10 * t:10 * t + 10, :]
    p4 = [send(snd.at[ring(x, s, 4)], r4.at[s - 1], dx(s)) for s in (1, 3, 2)]
    lm1.wait()
    lm2.wait()

    def adam(quarter, g):
        lane = cols(quarter)
        first_ref[:, lane] = 0.9 * m1[:, lane] + 0.1 * g
        second_ref[:, lane] = 0.95 * m2[:, lane] + 0.05 * g * g

    adam(x, snd[x, pl.ds(0, 10), :])
    for s, cp in zip((1, 3, 2), p4):
        cp.wait_recv()
        adam(ring(x, -s, 4), r4[s - 1, pl.ds(0, 10), :])
    for cp in sent:
        cp.wait_send()
    for odd in range(2):
        for i in (1, 2, 3):
            along_z(i, odd).wait_send()
    along_z(0, 1 - par).wait_send()
    assert count[0] <= zbase, count[0]


def on_device(*args):
    any_spec = pl.BlockSpec(memory_space=pl.ANY)
    V = pltpu.VMEM
    return pl.pallas_call(
        kernel,
        name="fused_layer",
        out_shape=(V((SEQ, D), BF), V((10, D), F32), V((10, D), F32)),
        in_specs=[any_spec] * 7,
        out_specs=(pl.BlockSpec(memory_space=V),) * 3,
        scratch_shapes=[
            V((SEQ, D), BF), V((SEQ, D), BF), V((SEQ, D), BF), V((SEQ, D), BF), V((SEQ, D), BF),
            V((SEQ, D), BF),
            V((D, SEQ), BF),
            V((2, 4, 160, SEQ), BF),
            V((2, 4, 2, 160, D), BF),
            V((2, 4, 160, D), BF),
            V((2, 4, 80, Q4), BF),
            V((2, 2, 4, 80, Q4), BF),
            V((2, 80, D), BF),
            V((2, 2, 80, D), BF),
            V((3, 2, 80, Q4), BF),
            V((3, 2, 80, Q4), BF),
            V((2, 160, Q4), BF),
            V((8, 48, Q4), BF),
            V((48, Q4), F32),
            V((4, 16, Q4), F32),
            V((3, 16, Q4), F32),
            V((10, D), F32), V((10, D), F32),
            pltpu.SemaphoreType.DMA((NSEM,)),
            pltpu.SemaphoreType.DMA((NSEM,)),
            pltpu.SemaphoreType.DMA((10,)),
        ],
        compiler_params=pltpu.CompilerParams(
            collective_id=0, has_side_effects=True, vmem_limit_bytes=60 * 2**20),
        cost_estimate=pl.CostEstimate(flops=15_000_000_000, bytes_accessed=14_000_000, transcendentals=2_600_000),
    )(*args)


def solution(mesh):
    rows = P(("blk", "rep"), None)
    return jax.shard_map(
        on_device, mesh=mesh, in_specs=(rows, rows, rows, rows, P("blk", None), rows, rows),
        out_specs=(rows, rows, rows), check_vma=False)
```

```python
import functools
import math

import jax
import jax.numpy as jnp
from jax import lax
from jax.experimental import pallas as pl
from jax.experimental.pallas import tpu as pltpu
from jax.sharding import PartitionSpec as P

HEADS = 20
HD = 128
SEQ = 448
D = 2560
NEG = -1e30
BF = jnp.bfloat16
F32 = jnp.float32
MESH = pl.DeviceIdType.MESH
WA, WB, WC = 32, 16, (64, 48)
Q4 = D // 4
NSEM = 160
CHUNKS = ((0, 48), (48, 32))
SCALE = math.log2(math.e) / math.sqrt(HD)
QBLOCKS = ((0, 256), (256, 192))


def ring(value, shift, size):
    return lax.rem(value + shift + size, size)


def kernel(q_hbm, k_hbm, v_hbm, t_hbm, w_hbm, m1_hbm, m2_hbm,
           out_ref, first_ref, second_ref,
           qs, ks, vs, ct, cto, ctx, ctt, cxo, wf, go, r1x, r2x, r1y, r2y, r3a, r3b, pc, rz, s3, snd, r4,
           m1, m2, ss, rs, ls):
    blk = lax.axis_index("blk")
    rep = lax.axis_index("rep")
    zh, y, c = blk // 8, lax.rem(blk // 2, 4), lax.rem(blk, 2)
    zl, x = rep // 4, lax.rem(rep, 4)
    z = zh * 4 + zl
    oz, oc = 1 - zh, 1 - c

    def at(xx, yy, zz, cc):
        return (zz // 4) * 8 + yy * 2 + cc, lax.rem(zz, 4) * 4 + xx

    def dx(s):
        return at(ring(x, s, 4), y, z, c)

    def dy(s):
        return at(x, ring(y, s, 4), z, c)

    def dz(s):
        return at(x, y, ring(z, s, 8), c)

    sib = at(x, y, z, oc)

    count = [0]
    sent = []

    def send(src, dst, dev):
        i = count[0]
        count[0] += 1
        cp = pltpu.make_async_remote_copy(
            src_ref=src, dst_ref=dst, send_sem=ss.at[i], recv_sem=rs.at[i],
            device_id=dev, device_id_type=MESH)
        cp.start()
        sent.append(cp)
        return cp

    def local(i, src, dst):
        cp = pltpu.make_async_copy(src, dst, ls.at[i])
        cp.start()
        return cp

    lw = local(0, w_hbm, wf.at[zh, y, c])
    lt = local(1, t_hbm, ct)
    lq = local(2, q_hbm, qs)
    lk = local(3, k_hbm, ks)
    lv = local(4, v_hbm, vs)
    lm1 = local(5, m1_hbm, m1)
    lm2 = local(6, m2_hbm, m2)

    lw.wait()
    barrier = pltpu.get_barrier_semaphore()
    partners = [dx(1), dx(2), dx(3), dy(1), dy(2), dy(3)] + [dz(s) for s in range(1, 8)] + [sib]
    for dev in partners:
        pl.semaphore_signal(barrier, inc=1, device_id=dev, device_id_type=MESH)
    pl.semaphore_wait(barrier, len(partners))

    def cols(quarter):
        return pl.ds(pl.multiple_of(quarter * Q4, 128), Q4)

    ra, rb = pl.ds(0, WA), pl.ds(WA, WB)
    rc = (pl.ds(WA + WB, WC[0]), pl.ds(WA + WB + WC[0], WC[1]))

    def give(dev, *region):
        ref = wf.at[region]
        return send(ref, ref, dev)

    a2o = [give(dy(s), zh, y, c, ra, cols(x)) for s in (1, 3, 2)]
    a1 = give(dz(4), zh, y, c, pl.ds(0, WA + WB), cols(x))
    c1 = [[give(dy(s), zh, y, c, rc[0], cols(zl)) for s in (1, 3, 2)]]
    b3o = [give(dy(1), zh, y, c, rb, pl.ds(0, D)), give(dy(3), zh, y, c, rb, pl.ds(0, D))]
    c1.append([give(dy(s), zh, y, c, rc[1], cols(zl)) for s in (1, 3, 2)])
    lt.wait()
    tsend = send(ct, cto, sib)
    lq.wait()
    lk.wait()
    lv.wait()

    def attend(i, carry):
        work = []
        for j in range(4):
            off = pl.multiple_of((i * 4 + j) * HD, HD)
            for q0, qn in QBLOCKS:
                work.append((off, pl.ds(off, HD), q0, qn, q0 + qn))
        scores = []
        for off, lane, q0, qn, kn in work:
            s = lax.dot_general(ks[pl.ds(0, kn), lane], qs[pl.ds(q0, qn), lane],
                                (((1,), (1,)), ((), ())), preferred_element_type=F32)
            later = lax.broadcasted_iota(jnp.int32, (qn, qn), 0) > lax.broadcasted_iota(
                jnp.int32, (qn, qn), 1)
            last = jnp.where(later, NEG, s[q0:])
            scores.append(jnp.concatenate([s[:q0], last], axis=0) if q0 else last)
        probs = []
        for s in scores:
            p = jnp.exp2((s - jnp.max(s, axis=0, keepdims=True)) * SCALE)
            probs.append((p.astype(BF), 1.0 / jnp.sum(p, axis=0, keepdims=True)))
        for (off, lane, q0, qn, kn), (p, inv) in zip(work, probs):
            o = inv * lax.dot_general(vs[pl.ds(0, kn), lane], p,
                                      (((0,), (0,)), ((), ())), preferred_element_type=F32)
            ctt[pl.ds(off, HD), pl.ds(q0, qn)] = o.astype(BF)
            ctx[pl.ds(q0, qn), lane] = o.T.astype(BF)
        return carry

    def heads(lo, hi):
        lax.fori_loop(lo // 4, hi // 4, attend, 0)

    def rows_of(zz, yy, cc):
        return pl.ds(pl.multiple_of((zz * 8 + yy * 2 + cc) * 160, 32), 160)

    every, both = pl.ds(0, 4), pl.ds(0, 2)
    halves = (pl.ds(0, D // 2), pl.ds(D // 2, D // 2))
    ah = (pl.ds(0, 2), pl.ds(2, 2))
    xp, xo, xm = ring(x, 1, 4), ring(x, 2, 4), ring(x, 3, 4)
    yp, yo, ym = ring(y, 1, 4), ring(y, 2, 4), ring(y, 3, 4)
    alld = pl.ds(0, D)
    sibs = []

    def zpos(s):
        zz = ring(z, s, 8)
        return zz // 4, lax.rem(zz, 4)

    c2 = [[], []]

    def zstep(step, strand):
        nxt = []
        for side in range(2):
            hh, ll = zpos(-step if side == 0 else step)
            if step:
                c2[strand][step - 1][side].wait_recv()
            if step < 4:
                part = ah[side] if step == 3 else every
                nxt.append(give(dz(1 if side == 0 else 7), hh, part, c, rc[strand], cols(ll)))
            if side == 0 or 0 < step < 4:
                if step < 4:
                    sibs.append(give(sib, hh, every, c, rc[strand], cols(ll)))
        if step == 4:
            hh, ll = zpos(4)
            sibs.append(give(sib, hh, every, c, rc[strand], cols(ll)))
        c2[strand].append(nxt)

    xs = []

    def context_across(blocks):
        for b in blocks:
            zz, yy = b // 4, b % 4
            xs.append(send(ctt.at[rows_of(zz, yy, oc)], cxo.at[zz, yy], sib))

    def grads(zz):
        for cp in xs[zz * 4:zz * 4 + 4]:
            cp.wait_recv()

        def tile(n, carry):
            lane = pl.ds(pl.multiple_of(n * 512, 128), 512)
            mine = jnp.concatenate([ctt[rows_of(zz, yy, c), :] for yy in range(4)], axis=0)
            acc = jnp.dot(mine, ct[:, lane], preferred_element_type=F32)
            acc += jnp.dot(cxo[zz].reshape(640, SEQ), cto[:, lane], preferred_element_type=F32)
            go[zz, :, :, lane] = acc.astype(BF).reshape(4, 160, 512)
            return carry

        lax.fori_loop(0, 5, tile, 0)

    def addf(*parts):
        total = parts[0].astype(F32)
        for part in parts[1:]:
            total = total + part.astype(F32)
        return total.astype(BF)

    s1, own, s2 = {}, {}, {}
    spans = [(pl.ds(lo, n), pl.ds(80 + lo, n)) for lo, n in CHUNKS]

    def first(k, zz):
        ga, gb = spans[k]
        fwd, back = (1, 3) if zz == 0 else (3, 1)
        bx, by = ring(x, back, 4), ring(y, back, 4)
        s1[k, zz] = (
            send(go.at[zz, every, ga, cols(xo)], r1x.at[zz, every, ga], dx(fwd)),
            send(go.at[zz, yo, gb, alld], r1y.at[zz, ga], dy(fwd)))
        own[k, zz] = (
            send(go.at[zz, every, ga, cols(bx)], r2x.at[1 - zz, zz, every, ga], dx(back)),
            send(go.at[zz, by, gb, alld], r2y.at[1 - zz, zz, ga], dy(back)))

    def second(k, zz):
        ga, gb = spans[k]
        fwd = 1 if zz == 0 else 3
        fx, fy = ring(x, fwd, 4), ring(y, fwd, 4)
        s1[k, zz][0].wait_recv()
        for yy in range(4):
            go[zz, yy, ga, cols(fx)] = addf(go[zz, yy, ga, cols(fx)], r1x[zz, yy, ga])
        a = send(go.at[zz, every, ga, cols(fx)], r2x.at[zz, zz, every, ga], dx(fwd))
        s1[k, zz][1].wait_recv()
        go[zz, fy, gb, :] = addf(go[zz, fy, gb, :], r1y[zz, ga])
        b = send(go.at[zz, fy, gb, alld], r2y.at[zz, zz, ga], dy(fwd))
        s2[k, zz] = (a, b)

    p2 = {}

    def third(k):
        ga, gb = spans[k]
        for zz in range(2):
            own[k, zz][0].wait_recv()
            s2[k, zz][0].wait_recv()
            for yy in range(4):
                go[zz, yy, ga, cols(x)] = addf(go[zz, yy, ga, cols(x)], r2x[0, zz, yy, ga], r2x[1, zz, yy, ga])
        pa = [send(go.at[both, ring(y, s, 4), ga, cols(x)], r3a.at[s - 1, both, ga], dy(s)) for s in (1, 3, 2)]
        for zz in range(2):
            own[k, zz][1].wait_recv()
            s2[k, zz][1].wait_recv()
            go[zz, y, gb, :] = addf(go[zz, y, gb, :], r2y[0, zz, ga], r2y[1, zz, ga])
        pb = [send(go.at[both, y, gb, cols(ring(x, s, 4))], r3b.at[s - 1, both, ga], dx(s)) for s in (1, 3, 2)]
        p2[k] = (pa, pb)

    def fourth(k):
        ga, gb = spans[k]
        for cp in p2[k][0]:
            cp.wait_recv()
        for zz in range(2):
            pc[zz, ga, :] = addf(go[zz, y, ga, cols(x)], *[r3a[s, zz, ga] for s in range(3)])
        for cp in p2[k][1]:
            cp.wait_recv()
        for zz in range(2):
            pc[zz, gb, :] = addf(go[zz, y, gb, cols(x)], *[r3b[s, zz, ga] for s in range(3)])

    par = lax.rem(z, 2)
    zbase = NSEM - 8

    def window(ll):
        return pl.ds(pl.multiple_of(ll * 40 - 8 * lax.rem(ll, 2), 16), 48)

    def along_z(i, odd):
        zz = lax.rem(z // 2 + i, 4) * 2 + odd
        hh, ll = zz // 4, lax.rem(zz, 4)
        slot = 2 * i + par
        return pltpu.make_async_remote_copy(
            src_ref=pc.at[hh, window(ll), :], dst_ref=rz.at[slot],
            send_sem=ss.at[zbase + 2 * i + odd], recv_sem=rs.at[zbase + slot],
            device_id=at(x, y, zz, c), device_id_type=MESH)

    def wave(odd):
        for i in (2, 1, 3):
            along_z(i, odd).start()

        @pl.when(par != odd)
        def _():
            along_z(0, odd).start()

    heads(0, 8)
    context_across([0, 1, 2])
    heads(8, 12)
    context_across([3])
    for cp in a2o:
        cp.wait_recv()
    a3o = [give(dx(1), zh, every, c, ra, cols(x)), give(dx(3), zh, every, c, ra, cols(x))]
    a1.wait_recv()
    a2t = [give(dy(s), oz, y, c, ra, cols(x)) for s in (1, 3, 2)]
    b2 = [give(dx(s), oz, y, c, rb, cols(x)) for s in (1, 3, 2)]
    tsend.wait_recv()
    grads(0)
    first(0, 0)
    first(1, 0)
    for strand in range(2):
        for cp in c1[strand]:
            cp.wait_recv()
        zstep(0, strand)
    heads(12, 20)
    context_across([4, 5, 6, 7])
    for cp in b2:
        cp.wait_recv()
    b3t = [give(dy(1), oz, y, c, rb, alld), give(dy(3), oz, y, c, rb, alld)]
    b3o[0].wait_recv()
    fo = [give(dy(1), zh, ym, c, rb, halves[0])]
    b3o[1].wait_recv()
    fo.append(give(dy(3), zh, yp, c, rb, halves[1]))
    grads(1)
    first(0, 1)
    for cp in a2t:
        cp.wait_recv()
    a3t = [give(dx(1), oz, every, c, ra, cols(x)), give(dx(3), oz, every, c, ra, cols(x))]
    zstep(1, 0)
    a3o[0].wait_recv()
    fa = [give(dx(1), zh, ah[0], c, ra, cols(xm))]
    a3o[1].wait_recv()
    fa.append(give(dx(3), zh, ah[1], c, ra, cols(xp)))
    second(0, 0)
    zstep(1, 1)
    second(0, 1)
    first(1, 1)
    for cp in b3t:
        cp.wait_recv()
    ft = [give(dy(1), oz, ym, c, rb, halves[0]), give(dy(3), oz, yp, c, rb, halves[1])]
    for cp in fo:
        cp.wait_recv()
    sibs.append(give(sib, zh, every, c, rb, alld))
    a3t[0].wait_recv()
    fa.append(give(dx(1), oz, ah[0], c, ra, cols(xm)))
    a3t[1].wait_recv()
    fa.append(give(dx(3), oz, ah[1], c, ra, cols(xp)))
    zstep(2, 0)
    second(1, 0)
    zstep(2, 1)
    second(1, 1)
    zstep(3, 0)
    third(0)
    for cp in ft:
        cp.wait_recv()
    sibs.append(give(sib, oz, every, c, rb, alld))
    for cp in fa:
        cp.wait_recv()
    sibs.append(give(sib, zh, every, c, ra, alld))
    sibs.append(give(sib, oz, every, c, ra, alld))
    zstep(3, 1)
    third(1)
    fourth(0)
    wave(0)
    zstep(4, 0)
    fourth(1)
    wave(1)
    zstep(4, 1)

    for cp in sibs:
        cp.wait_recv()
    for n in range(10):
        lane = pl.ds(n * 256, 256)
        w = wf[:, :, :, :, lane].reshape(D, 256)
        out_ref[:, lane] = jnp.dot(ctx[...], w, preferred_element_type=F32).astype(BF)

    for i in (1, 3, 2):
        for sender in range(2):
            pltpu.make_async_remote_copy(
                src_ref=rz.at[0], dst_ref=rz.at[2 * i + sender], send_sem=ss.at[zbase],
                recv_sem=rs.at[zbase + 2 * i + sender], device_id=dz(1), device_id_type=MESH).wait_recv()
    pltpu.make_async_remote_copy(
        src_ref=rz.at[0], dst_ref=rz.at[1 - par], send_sem=ss.at[zbase],
        recv_sem=rs.at[zbase + 1 - par], device_id=dz(1), device_id_type=MESH).wait_recv()
    total = pc[zh, window(zl), :].astype(F32) + rz[1 - par].astype(F32)
    for slot in range(2, 8):
        total = total + rz[slot].astype(F32)
    s3[...] = total

    mine = s3[pl.ds(pl.multiple_of(8 * lax.rem(zl, 2), 8), 40), :]
    snd[...] = jnp.zeros(snd.shape, F32)
    for t in range(4):
        snd[t, pl.ds(0, 10), :] = mine[10 * t:10 * t + 10, :]
    p4 = [send(snd.at[ring(x, s, 4)], r4.at[s - 1], dx(s)) for s in (1, 3, 2)]
    lm1.wait()
    lm2.wait()

    def adam(quarter, g):
        lane = cols(quarter)
        first_ref[:, lane] = 0.9 * m1[:, lane] + 0.1 * g
        second_ref[:, lane] = 0.95 * m2[:, lane] + 0.05 * g * g

    adam(x, snd[x, pl.ds(0, 10), :])
    for s, cp in zip((1, 3, 2), p4):
        cp.wait_recv()
        adam(ring(x, -s, 4), r4[s - 1, pl.ds(0, 10), :])
    for cp in sent:
        cp.wait_send()
    for odd in range(2):
        for i in (1, 2, 3):
            along_z(i, odd).wait_send()
    along_z(0, 1 - par).wait_send()
    assert count[0] <= zbase, count[0]


def on_device(*args):
    any_spec = pl.BlockSpec(memory_space=pl.ANY)
    V = pltpu.VMEM
    return pl.pallas_call(
        kernel,
        name="fused_layer",
        out_shape=(V((SEQ, D), BF), V((10, D), F32), V((10, D), F32)),
        in_specs=[any_spec] * 7,
        out_specs=(pl.BlockSpec(memory_space=V),) * 3,
        scratch_shapes=[
            V((SEQ, D), BF), V((SEQ, D), BF), V((SEQ, D), BF), V((SEQ, D), BF), V((SEQ, D), BF),
            V((SEQ, D), BF),
            V((D, SEQ), BF),
            V((2, 4, 160, SEQ), BF),
            V((2, 4, 2, 160, D), BF),
            V((2, 4, 160, D), BF),
            V((2, 4, 80, Q4), BF),
            V((2, 2, 4, 80, Q4), BF),
            V((2, 80, D), BF),
            V((2, 2, 80, D), BF),
            V((3, 2, 80, Q4), BF),
            V((3, 2, 80, Q4), BF),
            V((2, 160, Q4), BF),
            V((8, 48, Q4), BF),
            V((48, Q4), F32),
            V((4, 16, Q4), F32),
            V((3, 16, Q4), F32),
            V((10, D), F32), V((10, D), F32),
            pltpu.SemaphoreType.DMA((NSEM,)),
            pltpu.SemaphoreType.DMA((NSEM,)),
            pltpu.SemaphoreType.DMA((10,)),
        ],
        compiler_params=pltpu.CompilerParams(
            collective_id=0, has_side_effects=True, vmem_limit_bytes=60 * 2**20),
        cost_estimate=pl.CostEstimate(flops=15_000_000_000, bytes_accessed=14_000_000, transcendentals=2_600_000),
    )(*args)


def solution(mesh):
    rows = P(("blk", "rep"), None)
    return jax.shard_map(
        on_device, mesh=mesh, in_specs=(rows, rows, rows, rows, P("blk", None), rows, rows),
        out_specs=(rows, rows, rows), check_vma=False)
```
